768 devices in a mesh: dp: 32 (over y, z_lo), tensor: 24 (over x, z_hi, core).
Axes of the slice: x: 4, y: 8, z: 12 (z_hi: 3, z_lo: 4; z = z_hi * 4 + z_lo), core: 2. Of those that a mesh axis runs over, the one named last changes fastest.
Arguments:
- image_emb: float32 [196608, 1152], P(('dp', 'tensor')), may hold values from -6 to 6
- text_emb: float32 [196608, 1152], P(('dp', 'tensor')), may hold values from -6 to 6
- pooled: bfloat16 [196608, 1152], P(('dp', 'tensor')), may hold values from -1.25 to 1.25
- pairs: int32 [196608], P(('dp', 'tensor')), may hold values from 0 to 196607, as said below
- logit_scale: float32 [1], replicated, may hold values from 4 to 16
- logit_bias: float32 [1], replicated, may hold values from -3 to -1
Outputs:
- image_grad: float32 [196608, 1152], P(('dp', 'tensor'))
- weight_grad: float32 [1152, 1152], P('tensor')
The draws below stay inside these ranges and needn't reach their ends.
Inputs may be any that keep to these rules, and one draw needn't show every extreme that they name: pairs[i] lies in the window of row i; several images may share a positive text.
All inputs are finite; a program needn't handle non-finite values.
Results may differ from the reference program's by a relative error of at most 0.0052.
Values may be sent and summed in bfloat16 or wider, within the bound.
A program may use at most 32 MiB of HBM per device.

```python
import math
import jax
import jax.numpy as jnp
from jax import lax

D = 1152
ROWS = 256
BATCH = 196608
N_DP = 32
N_TENSOR = 24


def draw_pairs(key, part):
    key = jax.random.fold_in(key, 7)
    first_key, second_key = jax.random.split(key)
    total = ROWS * N_DP * N_TENSOR
    index = jnp.arange(total).astype(jnp.int32)
    owner = index // ROWS
    group = owner // N_TENSOR
    member = owner % N_TENSOR
    stops = jax.random.randint(first_key, (total,), 0, 4).astype(jnp.int32)
    offset = jax.random.randint(second_key, (total,), 0, ROWS).astype(jnp.int32)
    ends = (index == 0) | (index == total - 1)
    stops = jnp.where(ends, 1, stops).astype(jnp.int32)
    offset = jnp.where(index == 0, 0, offset).astype(jnp.int32)
    offset = jnp.where(index == total - 1, ROWS - 1, offset).astype(jnp.int32)
    target = (group + stops - 1 + N_DP) % N_DP * N_TENSOR + member
    return (target * ROWS + offset).astype(jnp.int32)


def with_spikes(entries, rng, source, target, parts, factor):
    def block_of(axis_at):
        return (jnp.arange(entries.shape[axis_at]) // (entries.shape[axis_at] // parts)).reshape((-1,) + (1,) * (entries.ndim - 1 - axis_at))

    one_side = jax.random.permutation(rng, parts)[block_of(target)]
    far = (block_of(target) + parts // 2) % parts
    return jnp.where((block_of(source) == one_side) | (block_of(source) == far), factor * entries, entries)


def block_levels(own_key, dims, shards, low, top_value):
    factor_of = 1.0
    for dim, parts in shards:
        heights = jax.random.uniform(jax.random.fold_in(jax.random.fold_in(own_key, 6), dim), (parts,), jnp.float32, low / len(shards), top_value / len(shards))
        factor_of = factor_of * jnp.repeat(jnp.exp(heights), dims[dim] // parts).reshape((-1,) + (1,) * (len(dims) - 1 - dim))
    return factor_of


def normal_values(stream_key, shape, spread, most, cuts=(), held_as=jnp.bfloat16):
    result = spread * jax.random.normal(stream_key, shape, jnp.float32)
    if cuts:
        result = result * block_levels(stream_key, shape, cuts, -0.22, 0.18)
    return jnp.clip(result, -most, most).astype(held_as)


def noise_with(rng, shape, scale, limit, shards, heavy, dtype=jnp.bfloat16):
    entries = scale * jax.random.normal(rng, shape, jnp.float32)
    if shards:
        entries = entries * block_levels(rng, shape, shards, -0.22, 0.18)
    return jnp.clip(with_spikes(entries, jax.random.fold_in(rng, 3), *heavy), -limit, limit).astype(dtype)


def setup_inputs(seed: int = 0) -> dict:
    seeds = jax.random.split(jax.random.key(seed), 7)
    image_emb = normal_values(seeds[0], (BATCH, D), 1.0, 6.0, ((0, 768),), jnp.float32)
    text_emb = normal_values(seeds[1], (BATCH, D), 1.0, 6.0, ((0, 768),), jnp.float32)
    pooled = noise_with(seeds[2], (BATCH, D), 0.05, 1.25, ((0, 768),), (0, 1, 384, 6.0))
    pairs = draw_pairs(jax.random.fold_in(seeds[6], 71), 0)
    logit_scale = jnp.clip(jnp.exp(jax.random.uniform(seeds[4], (1,), jnp.float32, math.log(4.0), math.log(16.0))), 4.0, 16.0)
    logit_bias = jnp.clip(jax.random.uniform(seeds[5], (1,), jnp.float32, -3.0, -1.0), -3.0, -1.0)
    return {"image_emb": image_emb, "text_emb": text_emb, "pooled": pooled, "pairs": pairs, "logit_scale": logit_scale, "logit_bias": logit_bias}


def reference(image_emb, text_emb, pooled, pairs, logit_scale, logit_bias):
    inv_img = lax.rsqrt(lax.optimization_barrier(jnp.sum(image_emb * image_emb, axis=1, keepdims=True)) + 1e-06)
    unit = image_emb * inv_img
    unit_copy = unit.astype(jnp.bfloat16)
    text_copy = (text_emb * lax.rsqrt(lax.optimization_barrier(jnp.sum(text_emb * text_emb, axis=1, keepdims=True)) + 1e-06)).astype(jnp.bfloat16)
    image_blocks = unit_copy.reshape(N_DP, N_TENSOR, ROWS, D)
    text_blocks = text_copy.reshape(N_DP, N_TENSOR, ROWS, D)
    pair_blocks = pairs.reshape(N_DP, N_TENSOR, ROWS)
    scale = logit_scale[0]
    bias = logit_bias[0]

    def one_group(group):
        pieces = [text_blocks[(group + offset) % N_DP] for offset in (-1, 0, 1, 2)]
        window = jnp.concatenate(pieces, axis=1).astype(jnp.float32)
        images = image_blocks[group].astype(jnp.float32)
        logits = scale * jnp.einsum('trd,tjd->trj', images, window) + bias
        owner = pair_blocks[group] // ROWS // N_TENSOR
        column = (owner - group + 1) % N_DP * ROWS + pair_blocks[group] % ROWS
        positions = jnp.arange(4 * ROWS).astype(jnp.int32)
        labels = (positions[None, None, :] == column[:, :, None]).astype(jnp.float32)
        coeff = (jax.nn.sigmoid(logits) - labels).astype(jnp.bfloat16)
        return scale * jnp.einsum('trj,tjd->trd', coeff.astype(jnp.float32), window)
    grad_unit = lax.map(one_group, jnp.arange(N_DP).astype(jnp.int32)).reshape(BATCH, D)
    image_grad = inv_img * (grad_unit - unit * lax.optimization_barrier(jnp.sum(unit * grad_unit, axis=1, keepdims=True)))
    cached = image_grad.astype(jnp.bfloat16)
    weight_grad = jnp.dot(pooled.T, cached, preferred_element_type=jnp.float32)
    return (image_grad, weight_grad)
```

```python
import functools

import jax
import jax.numpy as jnp
from jax import lax
from jax.experimental import pallas as pl
from jax.experimental.pallas import tpu as pltpu
from jax.sharding import PartitionSpec as P

X, ZH, Y, ZL = 4, 3, 8, 4
Z = ZH * ZL
H = 2
MESH = pl.DeviceIdType.MESH
BF16 = jnp.bfloat16
F32 = jnp.float32
TILE = (16, 128)


def kernel(
    image_hbm, text_hbm, pooled_hbm, column, scale_ref, bias_ref,
    grad_hbm, weight_out,
    image, text, pooled, unit, own, recv, total, grad, cached, cached_s,
    pt, pt_s, far_b, next_b, prev_b, next_f, prev_f,
    r1p, r1m, r2p, r2m, r3p, r3m,
    sum_f, sum_b, ry, vf, vb, rz, gathered,
    load_sem, t_send, t_recv, f_send, f_recv, x_send, x_recv,
    y_send, y_recv, z_send, z_recv, a_send, a_recv, b_send, b_recv,
):
    rows, width = image.shape
    step = rows // H
    cols = width // 128
    slab = width // (X * ZH * 2)
    ca = (cols + 1) // 2
    cb = cols - ca
    tall = slab // 16
    tiles = cols * tall

    dp = lax.axis_index("dp")
    t = lax.axis_index("tensor")
    y, p = dp // ZL, dp % ZL
    core = t % 2
    zh = (t // 2) % ZH
    x = t // (2 * ZH)
    z = zh * ZL + p

    def at(x_, y_, zh_, p_, core_):
        return (y_ * ZL + p_, (x_ * ZH + zh_) * 2 + core_)

    def z_dev(z_):
        return at(x, y, z_ // ZL, z_ % ZL, core)

    sibling = at(x, y, zh, p, 1 - core)
    x_next = at((x + 1) % X, y, zh, p, core)
    x_prev = at((x + X - 1) % X, y, zh, p, core)

    def remote(src, dst, send, recv_, device):
        return pltpu.make_async_remote_copy(
            src_ref=src, dst_ref=dst, send_sem=send, recv_sem=recv_,
            device_id=device, device_id_type=MESH,
        )

    load_text = pltpu.make_async_copy(text_hbm, text, load_sem.at[0])
    load_image = pltpu.make_async_copy(image_hbm, image, load_sem.at[1])
    load_pooled = pltpu.make_async_copy(pooled_hbm, pooled, load_sem.at[2])
    load_text.start()
    load_image.start()
    load_pooled.start()

    barrier = pltpu.get_barrier_semaphore()

    def greet(device):
        pl.semaphore_signal(barrier, inc=1, device_id=device, device_id_type=MESH)

    greet(at(x, (y + 1) % Y, zh, (p + ZL - 1) % ZL, core))
    greet(at(x, (y + Y - 1) % Y, zh, (p + 1) % ZL, core))
    greet(sibling)
    greet(x_next)
    greet(x_prev)

    @pl.loop(1, Y)
    def _(d):
        greet(at(x, (y + d) % Y, zh, p, core))

    @pl.loop(1, Z)
    def _(d):
        greet(z_dev((z + d) % Z))

    load_text.wait()
    for h in range(H):
        part = text[pl.ds(h * step, step), :]
        size = jnp.sum(part * part, axis=1, keepdims=True)
        own[h] = (part * lax.rsqrt(size + 1e-06)).astype(BF16)
    pl.semaphore_wait(barrier, 5 + (Y - 1) + (Z - 1))

    inner = jnp.logical_and(p >= 1, p <= 2)
    q_in = p - 1
    q_out = p // 3

    def text_copy(src, slot, h, send, y_, p_):
        return remote(
            src, recv.at[slot, h], t_send.at[send, h], t_recv.at[slot, h],
            at(x, y_, zh, p_, core),
        )

    def from_inner(which, h):
        q = q_in
        if which == 0:
            return text_copy(own.at[h], 1 - q, h, 0, y, 3 * q)
        if which == 1:
            return text_copy(own.at[h], q, h, 1, y, 2 - q)
        if which == 2:
            return text_copy(recv.at[1, h], 2, h, 2, y, q)
        if which == 3:
            return text_copy(recv.at[2, h], q, h, 3, (y + 1 - q) % Y, 3 * q)
        return text_copy(recv.at[0, h], 2, h, 4, (y + Y - 1) % Y, 2 + q)

    def from_outer(h):
        return text_copy(own.at[h], q_out, h, 0, y, 1 + q_out)

    @pl.when(inner)
    def _():
        for h in range(H):
            from_inner(0, h).start()
            from_inner(1, h).start()

    @pl.when(jnp.logical_not(inner))
    def _():
        for h in range(H):
            from_outer(h).start()

    load_pooled.wait()
    pt[...] = pooled[...].T.reshape(X * ZH, 2, slab, rows)
    pt_copy = remote(pt.at[:, 1 - core], pt_s, f_send.at[0], f_recv.at[0], sibling)
    pt_copy.start()

    scale = scale_ref[0]
    bias = bias_ref[0]
    load_image.wait()
    value = image[...]
    inv = lax.rsqrt(jnp.sum(value * value, axis=1, keepdims=True) + 1e-06)
    unit[...] = (value * inv).astype(BF16)
    sum_b[:, pl.ds(tiles, Y * ZL - tiles)] = jnp.zeros((ZH, Y * ZL - tiles, *TILE), BF16)

    def work(block, place, h):
        logits = lax.dot_general(
            unit[...], block, (((1,), (1,)), ((), ())), preferred_element_type=F32
        )
        logits = logits * scale + bias
        spot = lax.broadcasted_iota(jnp.int32, (rows, step), 1) + (place * rows + h * step)
        label = (spot == column[...]).astype(F32)
        coeff = (jax.nn.sigmoid(logits) - label).astype(BF16)
        return jnp.dot(coeff, block, preferred_element_type=F32)

    total[...] = work(own[0], 1, 0)
    for h in range(1, H):
        total[...] += work(own[h], 1, h)

    def arrive(slot, h):
        text_copy(recv.at[slot, h], slot, h, 0, y, p).wait_recv()

    first = jnp.where(p == 0, 1, 0)
    second = jnp.where(inner, 1, 2)
    third = jnp.where(p == 0, 0, jnp.where(p == 3, 1, 2))

    def take(slot, h, relay):
        arrive(slot, h)

        @pl.when(inner)
        def _():
            from_inner(relay, h).start()

        place = slot + jnp.minimum(slot, 1)
        total[...] += work(recv[slot, h], place, h)

    for h in range(H):
        take(first, h, 4)
        take(second, h, 2)
    for h in range(H):
        take(third, h, 3)

    def cached_copy(h):
        return remote(cached.at[h], cached_s.at[h], f_send.at[1 + h], f_recv.at[1 + h], sibling)

    def grad_copy(h):
        part = pl.ds(h * step, step)
        return pltpu.make_async_copy(grad.at[part], grad_hbm.at[part], load_sem.at[h])

    for h in range(H):
        part = pl.ds(h * step, step)
        value = image[part, :]
        inv = lax.rsqrt(jnp.sum(value * value, axis=1, keepdims=True) + 1e-06)
        line = value * inv
        full = scale * total[part, :]
        result = inv * (full - line * jnp.sum(line * full, axis=1, keepdims=True))
        grad[part, :] = result
        cached[h] = result.astype(BF16)
        cached_copy(h).start()
        grad_copy(h).start()

    pt_copy.wait_recv()
    for h in range(H):
        cached_copy(h).wait_recv()

    def product(x_):
        mine = pt[pl.ds(x_ * ZH, ZH), core].reshape(ZH * slab, rows)
        other = pt_s[pl.ds(x_ * ZH, ZH)].reshape(ZH * slab, rows)
        return jnp.dot(
            mine, cached[...].reshape(rows, width), preferred_element_type=F32
        ) + jnp.dot(other, cached_s[...].reshape(rows, width), preferred_element_type=F32)

    def block_of(value, c):
        return value[:, c * 128 : (c + 1) * 128].reshape(ZH, tall, *TILE)

    def x_copy(which, k):
        def go(src, dst, device):
            return remote(src, dst, x_send.at[which, k], x_recv.at[which, k], device)

        if which == 0:
            return go(far_b.at[k, pl.ds(0, ca)], r1p.at[k], x_next)
        if which == 1:
            return go(far_b.at[k, pl.ds(ca, cb)], r1m.at[k], x_prev)
        if which == 2:
            return go(next_b.at[k, pl.ds(ca, cb)], r2p.at[k], x_next)
        if which == 3:
            return go(prev_b.at[k, pl.ds(0, ca)], r2m.at[k], x_prev)
        if which == 4:
            return go(next_b.at[k, pl.ds(0, ca)], r3p.at[k], x_next)
        return go(prev_b.at[k, pl.ds(ca, cb)], r3m.at[k], x_prev)

    value = product((x + 2) % X)
    for c in range(cols):
        far_b[:, c] = block_of(value, c).astype(BF16)
    for k in range(ZH):
        x_copy(0, k).start()
        x_copy(1, k).start()
    value = product((x + 1) % X)
    for c in range(cols):
        if c < ca:
            next_f[:, c] = block_of(value, c)
        else:
            next_b[:, c] = block_of(value, c).astype(BF16)
    for k in range(ZH):
        x_copy(2, k).start()
    value = product((x + X - 1) % X)
    for c in range(cols):
        if c < ca:
            prev_b[:, c] = block_of(value, c).astype(BF16)
        else:
            prev_f[:, c - ca] = block_of(value, c)
    for k in range(ZH):
        x_copy(3, k).start()
    for k in range(ZH):
        x_copy(0, k).wait_recv()
        next_b[k, pl.ds(0, ca)] = (next_f[k] + r1p[k].astype(F32)).astype(BF16)
        x_copy(4, k).start()
        x_copy(1, k).wait_recv()
        prev_b[k, pl.ds(ca, cb)] = (prev_f[k] + r1m[k].astype(F32)).astype(BF16)
        x_copy(5, k).start()
    value = product(x)
    for c in range(cols):
        sum_f[:, pl.ds(c * tall, tall)] = block_of(value, c)

    def y_copy(k, d):
        to = (y + d) % Y
        return remote(
            sum_b.at[k, pl.ds(to * ZL, ZL)], ry.at[k, d - 1], y_send.at[k, d - 1],
            y_recv.at[k, d - 1], at(x, to, zh, p, core),
        )

    for k in range(ZH):
        x_copy(2, k).wait_recv()
        x_copy(3, k).wait_recv()
        x_copy(4, k).wait_recv()
        x_copy(5, k).wait_recv()
        low, high = pl.ds(0, ca * tall), pl.ds(ca * tall, cb * tall)
        left = r2m[k].astype(F32) + r3p[k].astype(F32)
        right = r2p[k].astype(F32) + r3m[k].astype(F32)
        value = sum_f[k, low] + left.reshape(ca * tall, *TILE)
        sum_f[k, low] = value
        sum_b[k, low] = value.astype(BF16)
        value = sum_f[k, high] + right.reshape(cb * tall, *TILE)
        sum_f[k, high] = value
        sum_b[k, high] = value.astype(BF16)

        @pl.loop(1, Y)
        def _(d):
            y_copy(k, d).start()

    for k in range(ZH):
        @pl.loop(1, Y)
        def _(d):
            y_copy(k, d).wait_recv()

        value = sum_f[k, pl.ds(y * ZL, ZL)]
        for d in range(Y - 1):
            value += ry[k, d].astype(F32)
        vf[pl.ds(k * ZL, ZL)] = value
        vb[pl.ds(k * ZL, ZL)] = value.astype(BF16)

    def z_copy(d):
        to = (z + d) % Z
        return remote(
            vb.at[to], rz.at[d - 1], z_send.at[d - 1], z_recv.at[d - 1], z_dev(to)
        )

    @pl.loop(1, Z)
    def _(d):
        z_copy(d).start()

    @pl.loop(1, Z)
    def _(d):
        z_copy(d).wait_recv()

    value = vf[z]
    for d in range(Z - 1):
        value += rz[d].astype(F32)
    gathered[y * ZL + p] = value.astype(BF16)

    def a_copy(d):
        mine = gathered.at[y * ZL + p]
        return remote(
            mine, mine, a_send.at[d - 1], a_recv.at[d - 1], at(x, y, zh, (p + d) % ZL, core)
        )

    def a_arrival(d):
        place = gathered.at[y * ZL + (p + ZL - d) % ZL]
        return remote(place, place, a_send.at[d - 1], a_recv.at[d - 1], sibling)

    def b_copy(d):
        mine = gathered.at[pl.ds(y * ZL, ZL)]
        return remote(
            mine, mine, b_send.at[d - 1], b_recv.at[d - 1], at(x, (y + d) % Y, zh, p, core)
        )

    def b_arrival(d):
        place = gathered.at[pl.ds((y + Y - d) % Y * ZL, ZL)]
        return remote(place, place, b_send.at[d - 1], b_recv.at[d - 1], sibling)

    @pl.loop(1, ZL)
    def _(d):
        a_copy(d).start()

    @pl.loop(1, ZL)
    def _(d):
        a_arrival(d).wait_recv()

    @pl.loop(1, Y)
    def _(d):
        b_copy(d).start()

    @pl.loop(1, Y)
    def _(d):
        b_arrival(d).wait_recv()

    for c in range(cols):
        for r in range(tall):
            weight_out[pl.ds(16 * r, 16), pl.ds(128 * c, 128)] = gathered[c * tall + r].astype(F32)

    @pl.when(inner)
    def _():
        for h in range(H):
            for which in range(5):
                from_inner(which, h).wait_send()

    @pl.when(jnp.logical_not(inner))
    def _():
        for h in range(H):
            from_outer(h).wait_send()

    pt_copy.wait_send()
    for h in range(H):
        cached_copy(h).wait_send()
        grad_copy(h).wait()
    for k in range(ZH):
        for which in range(6):
            x_copy(which, k).wait_send()

        @pl.loop(1, Y)
        def _(d):
            y_copy(k, d).wait_send()

    @pl.loop(1, Z)
    def _(d):
        z_copy(d).wait_send()

    @pl.loop(1, ZL)
    def _(d):
        a_copy(d).wait_send()

    @pl.loop(1, Y)
    def _(d):
        b_copy(d).wait_send()


def on_device(image_emb, text_emb, pooled, pairs, logit_scale, logit_bias):
    rows, width = image_emb.shape
    n_data = lax.axis_size("dp")
    n_group = lax.axis_size("tensor")
    slab = width // n_group
    step = rows // H
    cols = width // 128
    tall = slab // 16
    ca = (cols + 1) // 2
    cb = cols - ca
    owner = pairs // rows // n_group
    column = (owner - lax.axis_index("dp") + 1 + n_data) % n_data * rows + pairs % rows
    vmem = pltpu.VMEM
    dma = pltpu.SemaphoreType.DMA
    anywhere = pl.BlockSpec(memory_space=pl.ANY)
    in_vmem = pl.BlockSpec(memory_space=pltpu.VMEM)
    in_smem = pl.BlockSpec(memory_space=pltpu.SMEM)
    return pl.pallas_call(
        kernel,
        out_shape=(
            jax.ShapeDtypeStruct((rows, width), F32),
            jax.ShapeDtypeStruct((slab, width), F32),
        ),
        in_specs=[anywhere, anywhere, anywhere, in_vmem, in_smem, in_smem],
        out_specs=(anywhere, in_vmem),
        scratch_shapes=[
            vmem((rows, width), F32),
            vmem((rows, width), F32),
            vmem((rows, width), BF16),
            vmem((rows, width), BF16),
            vmem((H, step, width), BF16),
            vmem((3, H, step, width), BF16),
            vmem((rows, width), F32),
            vmem((rows, width), F32),
            vmem((H, step, width), BF16),
            vmem((H, step, width), BF16),
            vmem((X * ZH, 2, slab, rows), BF16),
            vmem((X * ZH, slab, rows), BF16),
            vmem((ZH, cols, tall, *TILE), BF16),
            vmem((ZH, cols, tall, *TILE), BF16),
            vmem((ZH, cols, tall, *TILE), BF16),
            vmem((ZH, ca, tall, *TILE), F32),
            vmem((ZH, cb, tall, *TILE), F32),
            vmem((ZH, ca, tall, *TILE), BF16),
            vmem((ZH, cb, tall, *TILE), BF16),
            vmem((ZH, cb, tall, *TILE), BF16),
            vmem((ZH, ca, tall, *TILE), BF16),
            vmem((ZH, ca, tall, *TILE), BF16),
            vmem((ZH, cb, tall, *TILE), BF16),
            vmem((ZH, Y * ZL, *TILE), F32),
            vmem((ZH, Y * ZL, *TILE), BF16),
            vmem((ZH, Y - 1, ZL, *TILE), BF16),
            vmem((Z, *TILE), F32),
            vmem((Z, *TILE), BF16),
            vmem((Z - 1, *TILE), BF16),
            vmem((Y * ZL, *TILE), BF16),
            dma((3,)),
            dma((5, H)), dma((3, H)),
            dma((1 + H,)), dma((1 + H,)),
            dma((6, ZH)), dma((6, ZH)),
            dma((ZH, Y - 1)), dma((ZH, Y - 1)),
            dma((Z - 1,)), dma((Z - 1,)),
            dma((ZL - 1,)), dma((ZL - 1,)),
            dma((Y - 1,)), dma((Y - 1,)),
        ],
        compiler_params=pltpu.CompilerParams(
            collective_id=0, has_side_effects=True, vmem_limit_bytes=48 * 1024 * 1024
        ),
        cost_estimate=pl.CostEstimate(
            flops=2 * rows * width * (8 * rows + width), bytes_accessed=10 * rows * width,
            transcendentals=0,
        ),
    )(image_emb, text_emb, pooled, column[:, None], logit_scale, logit_bias)


def solution(mesh):
    in_specs = (
        P(("dp", "tensor"), None),
        P(("dp", "tensor"), None),
        P(("dp", "tensor"), None),
        P(("dp", "tensor")),
        P(),
        P(),
    )
    out_specs = (P(("dp", "tensor"), None), P("tensor", None))
    return jax.shard_map(
        on_device, mesh=mesh, in_specs=in_specs, out_specs=out_specs, check_vma=False
    )
```
